32 devices in a mesh: row: 4 (over y, core), col: 4 (over z), feat: 2 (over x).
Axes of the slice: x: 2, y: 2, z: 4, core: 2. Of those that a mesh axis runs over, the one named last changes fastest.
Arguments:
- panel_student: bfloat16 [2048, 4096], P('row', 'feat'), may hold values from -0.01171875 to 0.01171875
- panel_teacher: bfloat16 [2048, 4096], P('row', 'feat'), may hold values from -0.01171875 to 0.01171875
- tokens_student: bfloat16 [3072, 4096], P('col', 'feat'), may hold values from -0.01171875 to 0.01171875
- tokens_teacher: bfloat16 [3072, 4096], P('col', 'feat'), may hold values from -0.01171875 to 0.01171875
Outputs:
- row_loss: float32 [2048], P(('row', 'col'))
- grad_panel: bfloat16 [2048, 4096], P(('row', 'col'), 'feat')
- grad_tokens: bfloat16 [3072, 4096], P('col', 'feat')
The draws below stay inside these ranges and needn't reach their ends.
All inputs are finite; a program needn't handle non-finite values.
Results may differ from the reference program's by a relative error of at most 0.0058.
Values may be sent and summed in bfloat16 or wider, within the bound.
A program may use at most 128 MiB of HBM per device.

```python
import jax
import jax.numpy as jnp
from jax import lax

D = 4096
PANEL = 2048
TOKENS = 3072


def block_levels(key, extent, shards, least, high):
    level, own = 1.0, jax.random.fold_in(key, 6)
    for position, parts in shards:
        draws = jnp.exp(jax.random.uniform(jax.random.fold_in(own, position), (parts,), jnp.float32, least / len(shards), high / len(shards)))
        level = level * jnp.repeat(draws, extent[position] // parts).reshape([-1 if axis == position else 1 for axis in range(len(extent))])
    return level


def noise(key, extent, spread, limit, cuts=(), held_as=jnp.bfloat16):
    array = spread * jax.random.normal(key, extent, jnp.float32)
    if cuts:
        array = array * block_levels(key, extent, cuts, -0.22, 0.18)
    return jnp.clip(array, -limit, limit).astype(held_as)


def setup_inputs(seed: int = 0) -> dict:
    keys = jax.random.split(jax.random.key(seed), 5)
    panel_student = noise(keys[0], (PANEL, D), 0.001953125, 0.01171875, ((0, 4), (1, 2)))
    panel_teacher = noise(keys[1], (PANEL, D), 0.001953125, 0.01171875, ((0, 4), (1, 2)))
    tokens_student = noise(keys[2], (TOKENS, D), 0.001953125, 0.01171875, ((0, 4), (1, 2)))
    tokens_teacher = noise(keys[3], (TOKENS, D), 0.001953125, 0.01171875, ((0, 4), (1, 2)))
    return dict(panel_student=panel_student, panel_teacher=panel_teacher, tokens_student=tokens_student, tokens_teacher=tokens_teacher)


epsilon = 1e-06

def inverse_norm(features):
    values = features.astype(jnp.float32)
    return 1.0 / jnp.sqrt(lax.optimization_barrier(jnp.sum(values * values, axis=1)) + epsilon)

def finish(term, unit, inverse):
    along = lax.optimization_barrier(jnp.sum(unit * term, axis=1))
    return ((term - unit * along[:, None]) * inverse[:, None]).astype(jnp.bfloat16)

def reference(panel_student, panel_teacher, tokens_student, tokens_teacher):
    inv_ps = inverse_norm(panel_student)
    inv_pt = inverse_norm(panel_teacher)
    inv_ts = inverse_norm(tokens_student)
    inv_tt = inverse_norm(tokens_teacher)
    student_gram = jnp.dot(panel_student, tokens_student.T, preferred_element_type=jnp.float32) * inv_ps[:, None] * inv_ts[None, :]
    teacher_gram = jnp.dot(panel_teacher, tokens_teacher.T, preferred_element_type=jnp.float32) * inv_pt[:, None] * inv_tt[None, :]
    mismatch = student_gram - teacher_gram
    row_loss = lax.optimization_barrier(jnp.sum(mismatch * mismatch, axis=1))
    doubled = (2.0 * mismatch).astype(jnp.bfloat16)
    panel_unit = panel_student.astype(jnp.float32) * inv_ps[:, None]
    token_unit = tokens_student.astype(jnp.float32) * inv_ts[:, None]
    panel_half = panel_unit.astype(jnp.bfloat16)
    token_half = token_unit.astype(jnp.bfloat16)
    panel_term = jnp.dot(doubled, token_half, preferred_element_type=jnp.float32)
    token_term = jnp.dot(doubled.T, panel_half, preferred_element_type=jnp.float32)
    grad_panel = finish(panel_term, panel_unit, inv_ps)
    grad_tokens = finish(token_term, token_unit, inv_tt * 0.0 + inv_ts)
    return (row_loss, grad_panel, grad_tokens)
```

```python
import functools

import jax
import jax.numpy as jnp
from jax import lax
from jax.experimental import pallas as pl
from jax.experimental.pallas import tpu as pltpu
from jax.sharding import PartitionSpec as P

epsilon = 1e-06
MESH = pl.DeviceIdType.MESH
f32, bf16 = jnp.float32, jnp.bfloat16
LANE = 128
CHUNK = 256


def nt(a, b):
    return lax.dot_general(a, b, (((1,), (1,)), ((), ())), preferred_element_type=f32)


def loop(count, body):
    def step(i, carry):
        body(i)
        return carry

    lax.fori_loop(0, count, step, 0)


def at(i, size):
    return pl.ds(pl.multiple_of(i * size, size), size)


def to_row(acc):
    rows = acc.shape[0]
    if rows < LANE:
        acc = jnp.concatenate([acc, jnp.zeros((LANE - rows, LANE), f32)], axis=0)
    return jnp.sum(acc.T, axis=0, keepdims=True)


def to_column(row):
    return jnp.broadcast_to(row, (LANE, row.shape[1])).T


def kernel(
    rows_n, cols_n,
    ps_h, pt_h, ts_h, tt_h,
    loss_o, gp_o, gt_o,
    ps, pt, ts, tt, ph, th,
    sq, sqr, inv, psc, ptc, tsc,
    m1, g1t, m2, xs1, xr1, xs2, xr2, d_all, dts,
    loss_acc, lsend, lrecv,
    part, zs, zr, zl,
    tpart, cs, cr, ys, yr,
    als, alr,
    lsem, sqsem, x1sem, x2s, x2r, cos, cor, yos, yor, zss, zrr, zlr, los, lor, als_s, alr_s, ags, agr, outs,
):
    N = cols_n
    Pn, F = ps.shape
    T = ts.shape[0]
    C = T // CHUNK
    rp = Pn // N
    nr = Pn - rp
    row, col, feat = lax.axis_index("row"), lax.axis_index("col"), lax.axis_index("feat")
    xdev = {"feat": 1 - feat}
    low = row % 2
    cdev = {"row": row + 1 - 2 * low}
    ydev = {"row": row + 2 - 4 * ((row // 2) % 2)}
    first_half = col < N // 2
    r1 = pl.multiple_of(jnp.where(first_half, N - 1, 0) * rp, rp)
    r2 = pl.multiple_of(jnp.where(first_half, 0, 1) * rp, rp)
    HC = CHUNK // 2

    loads = [
        pltpu.make_async_copy(h, v, lsem.at[i])
        for i, (h, v) in enumerate(((ps_h, ps), (ts_h, ts), (pt_h, pt), (tt_h, tt)))
    ]
    for load in loads:
        load.start()

    barrier = pltpu.get_barrier_semaphore()
    for dev in (xdev, cdev, ydev):
        pl.semaphore_signal(barrier, inc=1, device_id=dev, device_id_type=MESH)
    for k in range(1, N):
        pl.semaphore_signal(barrier, inc=1, device_id={"col": (col + k) % N}, device_id_type=MESH)
    pl.semaphore_wait(barrier, 3 + N - 1)

    def remote(src, dst, s, r, dev):
        return pltpu.make_async_remote_copy(
            src_ref=src, dst_ref=dst, send_sem=s, recv_sem=r, device_id=dev, device_id_type=MESH
        )

    sq[...] = jnp.zeros_like(sq)

    def squares(ref, i, count):
        def body(t):
            acc = jnp.zeros((LANE, LANE), f32)
            for k in range(F // LANE):
                v = ref[at(t, LANE), k * LANE:(k + 1) * LANE].astype(f32)
                acc = acc + v * v
            sq[i:i + 1, at(t, LANE)] = to_row(acc)

        loop(count // LANE, body)

    for load, (ref, i, count) in zip(loads, ((ps, 0, Pn), (ts, 2, T), (pt, 1, Pn), (tt, 3, T))):
        load.wait()
        squares(ref, i, count)
    sq_copy = remote(sq, sqr, sqsem.at[0], sqsem.at[1], xdev)
    sq_copy.start()

    def raw(c):
        m1[c] = nt(ps[pl.ds(r1, rp), :], ts[at(c, CHUNK), :])
        g1t[c] = nt(pt[pl.ds(r1, rp), :], tt[at(c, CHUNK), :])

    loop(C, raw)
    sq_copy.wait_recv()
    inv[...] = 1.0 / jnp.sqrt(sq[...] + sqr[...] + epsilon)
    for i, ref in ((0, psc), (1, ptc), (2, tsc)):
        for t in range(ref.shape[0] // LANE):
            ref[t * LANE:(t + 1) * LANE, :] = to_column(inv[i:i + 1, t * LANE:(t + 1) * LANE])

    def scaled(gs, gt, c, r0, count, m_ref, s_ref):
        for j in range(CHUNK // LANE):
            lanes = slice(j * LANE, (j + 1) * LANE)
            where = pl.ds(pl.multiple_of(c * CHUNK + j * LANE, LANE), LANE)
            m = gs[:, lanes] * psc[pl.ds(r0, count), :] * inv[2:3, where]
            m = m - gt[:, lanes] * ptc[pl.ds(r0, count), :] * inv[3:4, where]
            m_ref[c, :, lanes] = m
            s_ref[c, :, lanes] = m.astype(bf16)

    loop(C, lambda c: scaled(m1[c], g1t[c], c, r1, rp, m1, xs1))
    x1_copy = remote(xs1, xr1, x1sem.at[0], x1sem.at[1], xdev)
    x1_copy.start()

    def x2_copy(c):
        return remote(xs2.at[c], xr2.at[c], x2s.at[c], x2r.at[c], xdev)

    def rest(c):
        gs = nt(ps[pl.ds(r2, nr), :], ts[at(c, CHUNK), :])
        gt = nt(pt[pl.ds(r2, nr), :], tt[at(c, CHUNK), :])
        scaled(gs, gt, c, r2, nr, m2, xs2)
        x2_copy(c).start()

    loop(C, rest)

    def halves(src, column, dst):
        def body(t):
            scale = column[at(t, LANE), :]
            for k in range(F // LANE):
                lanes = slice(k * LANE, (k + 1) * LANE)
                dst[at(t, LANE), lanes] = (src[at(t, LANE), lanes].astype(f32) * scale).astype(bf16)

        loop(src.shape[0] // LANE, body)

    halves(ts, tsc, th)
    halves(ps, psc, ph)

    loss_acc[...] = jnp.zeros_like(loss_acc)

    def settle(m_ref, x_ref, c, r0, count):
        for j in range(CHUNK // LANE):
            lanes = slice(j * LANE, (j + 1) * LANE)
            m = m_ref[c, :, lanes] + x_ref[c, :, lanes].astype(f32)
            where = pl.ds(pl.multiple_of(c * CHUNK + j * LANE, LANE), LANE)
            d_all[pl.ds(r0, count), where] = (2.0 * m).astype(bf16)
            loss_acc[pl.ds(r0, count), :] += m * m

    def panel_product(r0, count):
        def body(n):
            part[pl.ds(r0, count), at(n, CHUNK)] = jnp.dot(
                d_all[pl.ds(r0, count), :], th[:, at(n, CHUNK)], preferred_element_type=f32
            )

        loop(F // CHUNK, body)

    def block(d):
        return pl.ds(pl.multiple_of(d * rp, rp), rp)

    def right(d):
        return remote(zs.at[block(d), :], zr.at[block(d), :], zss.at[d], zrr.at[d], {"col": (col + 1) % N})

    def left(d):
        return remote(zs.at[block(d), :], zl.at[block(d), :], zss.at[d], zlr.at[d], {"col": (col + N - 1) % N})

    def forward(d, copy, arrived):
        def body(n):
            value = part[block(d), at(n, CHUNK)]
            if arrived is not None:
                value = value + arrived[block(d), at(n, CHUNK)].astype(f32)
            zs[block(d), at(n, CHUNK)] = value.astype(bf16)

        if arrived is not None:
            copy(d).wait_recv()
        loop(F // CHUNK, body)
        copy(d).start()

    x1_copy.wait_recv()
    loop(C, lambda c: settle(m1, xr1, c, r1, rp))
    panel_product(r1, rp)

    @pl.when(col == 0)
    def _():
        forward(N - 1, right, None)

    @pl.when(col == N - 1)
    def _():
        forward(0, left, None)

    def core_copy(c):
        return remote(cs.at[c], cr.at[c], cos.at[c], cor.at[c], cdev)

    def y_copy(c):
        return remote(ys.at[c], yr.at[c], yos.at[c], yor.at[c], ydev)

    mine = pl.ds(pl.multiple_of(low * HC, HC), HC)
    other = pl.ds(pl.multiple_of((1 - low) * HC, HC), HC)

    def token_product(c):
        dts[...] = d_all[:, at(c, CHUNK)].T

        def body(n):
            tpart[:, at(n, CHUNK)] = jnp.dot(dts[...], ph[:, at(n, CHUNK)], preferred_element_type=f32)
            cs[c, :, at(n, CHUNK)] = tpart[other, at(n, CHUNK)].astype(bf16)

        loop(F // CHUNK, body)
        core_copy(c).start()
        core_copy(c).wait_recv()

        def add(n):
            value = tpart[mine, at(n, CHUNK)] + cr[c, :, at(n, CHUNK)].astype(f32)
            ys[c, :, at(n, CHUNK)] = value.astype(bf16)

        loop(F // CHUNK, add)
        y_copy(c).start()

    def arrive(c):
        x2_copy(c).wait_recv()
        settle(m2, xr2, c, r2, nr)

    def both(c):
        arrive(c)
        token_product(c)

    loop(C - 1, both)
    arrive(C - 1)
    panel_product(r2, nr)

    @pl.when(col == 0)
    def _():
        for d in range(N - 2, 0, -1):
            forward(d, right, None)

    @pl.when(col == N - 1)
    def _():
        for d in range(1, N - 1):
            forward(d, left, None)

    @pl.when((col > 0) & (col < N // 2))
    def _():
        forward(N - 1, right, zr)

    @pl.when((col < N - 1) & (col >= N // 2))
    def _():
        forward(0, left, zl)

    token_product(C - 1)

    def loss_copy(d, src):
        return remote(lsend.at[d], lrecv.at[src], los.at[d], lor.at[src], {"col": d})

    def loss_rows(d):
        lsend[d] = jnp.broadcast_to(to_row(loss_acc[block(d), :]), lsend.shape[1:])

    loop(N, loss_rows)
    for k in range(1, N):
        d = (col + k) % N
        loss_copy(d, col).start()

    def along_copy(i):
        return remote(als.at[i], alr.at[i], als_s.at[i], alr_s.at[i], xdev)

    def token_rows(c):
        return pl.ds(pl.multiple_of(c * CHUNK + low * HC, HC), HC)

    def token_term(c, lanes):
        return ys[c, :, lanes].astype(f32) + yr[c, :, lanes].astype(f32)

    def token_along(c):
        y_copy(c).wait_recv()
        scale = tsc[token_rows(c), :]
        acc = jnp.zeros((HC, LANE), f32)
        for k in range(F // LANE):
            lanes = slice(k * LANE, (k + 1) * LANE)
            acc = acc + ts[token_rows(c), lanes].astype(f32) * scale * token_term(c, lanes)
        als[c] = jnp.broadcast_to(to_row(acc), als.shape[1:])
        along_copy(c).start()

    def gather_copy(c):
        return remote(cr.at[c], gt_o.at[token_rows(c), :], ags.at[c], agr.at[c], cdev)

    def own_copy(c):
        return pltpu.make_async_copy(cr.at[c], gt_o.at[token_rows(c), :], outs.at[c])

    def token_finish(c):
        along_copy(c).wait_recv()
        along = to_column(als[c, 0:1, :] + alr[c, 0:1, :])
        scale = tsc[token_rows(c), :]
        for k in range(F // LANE):
            lanes = slice(k * LANE, (k + 1) * LANE)
            unit = ts[token_rows(c), lanes].astype(f32) * scale
            cr[c, :, lanes] = ((token_term(c, lanes) - unit * along) * scale).astype(bf16)
        gather_copy(c).start()
        own_copy(c).start()

    def chain(k):
        d = N - 1 - k
        go = (col < d) & (col > 0)
        if k == 0:
            go = go & (col >= N // 2)

        @pl.when(go)
        def _():
            forward(d, right, zr)

        e = k
        go = (col > e) & (col < N - 1)
        if k == 0:
            go = go & (col < N // 2)

        @pl.when(go)
        def _():
            forward(e, left, zl)

    for i in range(max(C, N - 1)):
        if i < N - 1:
            chain(i)
        if i < C:
            token_along(i)
        if 0 < i < C:
            token_finish(i - 1)

    own = block(col)

    def absorb(arrived):
        def body(n):
            part[own, at(n, CHUNK)] += arrived[own, at(n, CHUNK)].astype(f32)

        loop(F // CHUNK, body)

    @pl.when(col > 0)
    def _():
        right(col).wait_recv()
        absorb(zr)

    @pl.when(col < N - 1)
    def _():
        left(col).wait_recv()
        absorb(zl)

    scale = psc[own, :]
    acc = jnp.zeros((rp, LANE), f32)
    for k in range(F // LANE):
        lanes = slice(k * LANE, (k + 1) * LANE)
        acc = acc + ps[own, lanes].astype(f32) * scale * part[own, lanes]
    als[C] = jnp.broadcast_to(to_row(acc), als.shape[1:])
    along_copy(C).start()
    token_finish(C - 1)
    total = lsend[col]
    for k in range(1, N):
        src = (col + N - k) % N
        loss_copy(col, src).wait_recv()
        total = total + lrecv[src]
    loss_o[...] = total
    along_copy(C).wait_recv()
    along = to_column(als[C, 0:1, :] + alr[C, 0:1, :])[:rp]
    for k in range(F // LANE):
        lanes = slice(k * LANE, (k + 1) * LANE)
        unit = ps[own, lanes].astype(f32) * scale
        gp_o[:, lanes] = ((part[own, lanes] - unit * along) * scale).astype(bf16)

    sq_copy.wait_send()
    x1_copy.wait_send()

    def ends(c):
        x2_copy(c).wait_send()
        core_copy(c).wait_send()
        y_copy(c).wait_send()
        along_copy(c).wait_send()
        gather_copy(c).wait_send()
        gather_copy(c).wait_recv()
        own_copy(c).wait()

    loop(C, ends)
    along_copy(C).wait_send()

    for k in range(1, N):
        d = (col + k) % N
        loss_copy(d, col).wait_send()
        right(d).wait_send()


def local(rows_n, cols_n, panel_student, panel_teacher, tokens_student, tokens_teacher):
    Pn, F = panel_student.shape
    T = tokens_student.shape[0]
    N, C = cols_n, T // CHUNK
    rp = Pn // N
    nr, HC, W = Pn - rp, CHUNK // 2, max(Pn, T)
    lp = max(rp, LANE)
    V, S = pltpu.VMEM, pltpu.SemaphoreType.DMA
    scratch = [
        V((Pn, F), bf16), V((Pn, F), bf16), V((T, F), bf16), V((T, F), bf16), V((Pn, F), bf16), V((T, F), bf16),
        V((8, W), f32), V((8, W), f32), V((8, W), f32), V((Pn, LANE), f32), V((Pn, LANE), f32), V((T, LANE), f32),
        V((C, rp, CHUNK), f32), V((C, rp, CHUNK), f32), V((C, nr, CHUNK), f32),
        V((C, rp, CHUNK), bf16), V((C, rp, CHUNK), bf16), V((C, nr, CHUNK), bf16), V((C, nr, CHUNK), bf16),
        V((Pn, T), bf16), V((CHUNK, Pn), bf16),
        V((Pn, LANE), f32), V((N, 8, lp), f32), V((N, 8, lp), f32),
        V((Pn, F), f32), V((Pn, F), bf16), V((Pn, F), bf16), V((Pn, F), bf16),
        V((CHUNK, F), f32), V((C, HC, F), bf16), V((C, HC, F), bf16), V((C, HC, F), bf16), V((C, HC, F), bf16),
        V((C + 1, 8, lp), f32), V((C + 1, 8, lp), f32),
        S((4,)), S((2,)), S((2,)), S((C,)), S((C,)), S((C,)), S((C,)), S((C,)), S((C,)),
        S((N,)), S((N,)), S((N,)), S((N,)), S((N,)), S((C + 1,)), S((C + 1,)), S((C,)), S((C,)), S((C,)),
    ]
    anywhere, vmem = pl.BlockSpec(memory_space=pl.ANY), pl.BlockSpec(memory_space=pltpu.VMEM)
    loss, grad_panel, grad_tokens = pl.pallas_call(
        functools.partial(kernel, rows_n, cols_n),
        out_shape=(
            jax.ShapeDtypeStruct((8, lp), f32),
            jax.ShapeDtypeStruct((rp, F), bf16),
            jax.ShapeDtypeStruct((T, F), bf16),
        ),
        in_specs=[anywhere] * 4,
        out_specs=(vmem, vmem, anywhere),
        scratch_shapes=scratch,
        compiler_params=pltpu.CompilerParams(
            collective_id=0, has_side_effects=True, vmem_limit_bytes=62 * 1024 * 1024
        ),
    )(panel_student, panel_teacher, tokens_student, tokens_teacher)
    return loss[0, :rp], grad_panel, grad_tokens


def solution(mesh):
    placed = (P("row", "feat"), P("row", "feat"), P("col", "feat"), P("col", "feat"))
    return jax.shard_map(
        functools.partial(local, mesh.shape["row"], mesh.shape["col"]),
        mesh=mesh,
        in_specs=placed,
        out_specs=(P(("row", "col")), P(("row", "col"), "feat"), P("col", "feat")),
        check_vma=False,
    )
```

```python
import functools

import jax
import jax.numpy as jnp
from jax import lax
from jax.experimental import pallas as pl
from jax.experimental.pallas import tpu as pltpu
from jax.sharding import PartitionSpec as P

epsilon = 1e-06
MESH = pl.DeviceIdType.MESH
f32, bf16 = jnp.float32, jnp.bfloat16
LANE = 128
CHUNK = 256
TILE = 1024


def nt(a, b):
    return lax.dot_general(a, b, (((1,), (1,)), ((), ())), preferred_element_type=f32)


def loop(count, body):
    def step(i, carry):
        body(i)
        return carry

    lax.fori_loop(0, count, step, 0)


def at(i, size):
    return pl.ds(pl.multiple_of(i * size, size), size)


def to_row(acc):
    rows = acc.shape[0]
    if rows < LANE:
        acc = jnp.concatenate([acc, jnp.zeros((LANE - rows, LANE), f32)], axis=0)
    return jnp.sum(acc.T, axis=0, keepdims=True)


def to_column(row):
    return jnp.broadcast_to(row, (LANE, row.shape[1])).T


def kernel(
    rows_n, cols_n,
    ps_h, pt_h, ts_h, tt_h,
    loss_o, gp_o, gt_o,
    ps, pt, ts, tt, ph, th,
    sq, sqr, inv, psc, ptc, tsc,
    m1, g1t, g2t, m2, xs1, xr1, xs2, xr2, d_all, dts,
    loss_acc, lsend, lrecv,
    part, zs, zr, zl,
    tpart, cs, cr, ys, yr,
    als, alr,
    lsem, sqsem, x1sem, x2s, x2r, cos, cor, yos, yor, zss, zrr, zlr, los, lor, als_s, alr_s, ags, agr, outs,
):
    N = cols_n
    Pn, F = ps.shape
    T = ts.shape[0]
    C = T // CHUNK
    rp = Pn // N
    nr = Pn - rp
    row, col, feat = lax.axis_index("row"), lax.axis_index("col"), lax.axis_index("feat")
    xdev = {"feat": 1 - feat}
    low = row % 2
    cdev = {"row": row + 1 - 2 * low}
    across = row + 2 - 4 * ((row // 2) % 2)
    ydev = {"row": across}
    xydev = {"row": across, "feat": 1 - feat}
    first_half = col < N // 2
    r1 = pl.multiple_of(jnp.where(first_half, N - 1, 0) * rp, rp)
    r2 = pl.multiple_of(jnp.where(first_half, 0, 1) * rp, rp)
    HC = CHUNK // 2

    loads = [
        pltpu.make_async_copy(h, v, lsem.at[i])
        for i, (h, v) in enumerate(((ps_h, ps), (ts_h, ts), (pt_h, pt), (tt_h, tt)))
    ]
    for load in loads:
        load.start()

    barrier = pltpu.get_barrier_semaphore()
    for dev in (xdev, cdev, ydev, xydev):
        pl.semaphore_signal(barrier, inc=1, device_id=dev, device_id_type=MESH)
    for k in range(1, N):
        pl.semaphore_signal(barrier, inc=1, device_id={"col": (col + k) % N}, device_id_type=MESH)
    pl.semaphore_wait(barrier, 4 + N - 1)

    def remote(src, dst, s, r, dev):
        return pltpu.make_async_remote_copy(
            src_ref=src, dst_ref=dst, send_sem=s, recv_sem=r, device_id=dev, device_id_type=MESH
        )

    sq[...] = jnp.zeros_like(sq)

    def squares(ref, i, count):
        def body(t):
            acc = jnp.zeros((LANE, LANE), f32)
            for k in range(F // LANE):
                v = ref[at(t, LANE), k * LANE:(k + 1) * LANE].astype(f32)
                acc = acc + v * v
            sq[i:i + 1, at(t, LANE)] = to_row(acc)

        loop(count // LANE, body)

    for load, (ref, i, count) in zip(loads, ((ps, 0, Pn), (ts, 2, T), (pt, 1, Pn), (tt, 3, T))):
        load.wait()
        squares(ref, i, count)
    sq_copy = remote(sq, sqr, sqsem.at[0], sqsem.at[1], xdev)
    sq_copy.start()

    first = slice(0, CHUNK)
    m1[0] = nt(ps[pl.ds(r1, rp), :], ts[first, :])
    m2[0] = nt(ps[pl.ds(r2, nr), :], ts[first, :])
    g1t[...] = nt(pt[pl.ds(r1, rp), :], tt[first, :])
    g2t[...] = nt(pt[pl.ds(r2, nr), :], tt[first, :])
    sq_copy.wait_recv()
    inv[...] = 1.0 / jnp.sqrt(sq[...] + sqr[...] + epsilon)
    for i, ref in ((0, psc), (1, ptc), (2, tsc)):
        for t in range(ref.shape[0] // LANE):
            ref[t * LANE:(t + 1) * LANE, :] = to_column(inv[i:i + 1, t * LANE:(t + 1) * LANE])

    def scaled(gs, gt, c, r0, count, m_ref, s_ref):
        for j in range(CHUNK // LANE):
            lanes = slice(j * LANE, (j + 1) * LANE)
            where = pl.ds(pl.multiple_of(c * CHUNK + j * LANE, LANE), LANE)
            m = gs[:, lanes] * psc[pl.ds(r0, count), :] * inv[2:3, where]
            m = m - gt[:, lanes] * ptc[pl.ds(r0, count), :] * inv[3:4, where]
            m_ref[c, :, lanes] = m
            s_ref[c, :, lanes] = m.astype(bf16)

    def x2_copy(c):
        return remote(xs2.at[c], xr2.at[c], x2s.at[c], x2r.at[c], xdev)

    x0_copy = remote(xs1.at[0], xr1.at[0], x1sem.at[2], x1sem.at[3], xdev)
    later = pl.ds(1, C - 1)
    x1_copy = remote(xs1.at[later], xr1.at[later], x1sem.at[0], x1sem.at[1], xdev)

    scaled(m2[0], g2t[...], 0, r2, nr, m2, xs2)
    x2_copy(0).start()
    scaled(m1[0], g1t[...], 0, r1, rp, m1, xs1)
    x0_copy.start()

    def top(i):
        c = i + 1
        gs = nt(ps[pl.ds(r1, rp), :], ts[at(c, CHUNK), :])
        gt = nt(pt[pl.ds(r1, rp), :], tt[at(c, CHUNK), :])
        scaled(gs, gt, c, r1, rp, m1, xs1)

    loop(C - 1, top)
    x1_copy.start()

    def rest(i):
        c = i + 1
        gs = nt(ps[pl.ds(r2, nr), :], ts[at(c, CHUNK), :])
        gt = nt(pt[pl.ds(r2, nr), :], tt[at(c, CHUNK), :])
        scaled(gs, gt, c, r2, nr, m2, xs2)
        x2_copy(c).start()

    loop(C - 1, rest)

    def halves(src, column, dst):
        def body(t):
            scale = column[at(t, LANE), :]
            for k in range(F // LANE):
                lanes = slice(k * LANE, (k + 1) * LANE)
                dst[at(t, LANE), lanes] = (src[at(t, LANE), lanes].astype(f32) * scale).astype(bf16)

        loop(src.shape[0] // LANE, body)

    halves(ts, tsc, th)
    halves(ps, psc, ph)

    loss_acc[...] = jnp.zeros_like(loss_acc)

    def settle(m_ref, x_ref, c, r0, count):
        for j in range(CHUNK // LANE):
            lanes = slice(j * LANE, (j + 1) * LANE)
            m = m_ref[c, :, lanes] + x_ref[c, :, lanes].astype(f32)
            where = pl.ds(pl.multiple_of(c * CHUNK + j * LANE, LANE), LANE)
            d_all[pl.ds(r0, count), where] = (2.0 * m).astype(bf16)
            loss_acc[pl.ds(r0, count), :] += m * m

    def panel_product(r0, count):
        def body(n):
            part[pl.ds(r0, count), at(n, TILE)] = jnp.dot(
                d_all[pl.ds(r0, count), :], th[:, at(n, TILE)], preferred_element_type=f32
            )

        loop(F // TILE, body)

    def block(d):
        return pl.ds(pl.multiple_of(d * rp, rp), rp)

    def right(d):
        return remote(zs.at[block(d), :], zr.at[block(d), :], zss.at[d], zrr.at[d], {"col": (col + 1) % N})

    def left(d):
        return remote(zs.at[block(d), :], zl.at[block(d), :], zss.at[d], zlr.at[d], {"col": (col + N - 1) % N})

    def forward(d, copy, arrived):
        def body(n):
            value = part[block(d), at(n, CHUNK)]
            if arrived is not None:
                value = value + arrived[block(d), at(n, CHUNK)].astype(f32)
            zs[block(d), at(n, CHUNK)] = value.astype(bf16)

        if arrived is not None:
            copy(d).wait_recv()
        loop(F // CHUNK, body)
        copy(d).start()

    def core_copy(c):
        return remote(cs.at[c], cr.at[c], cos.at[c], cor.at[c], cdev)

    def y_copy(c):
        return remote(ys.at[c], yr.at[c], yos.at[c], yor.at[c], ydev)

    mine = pl.ds(pl.multiple_of(low * HC, HC), HC)
    other = pl.ds(pl.multiple_of((1 - low) * HC, HC), HC)

    def along_copy(c, i):
        return remote(als.at[c], alr.at[c, i], als_s.at[c, i], alr_s.at[c, i], (xdev, ydev, xydev)[i])

    def token_rows(c):
        return pl.ds(pl.multiple_of(c * CHUNK + low * HC, HC), HC)

    def token_product(c):
        dts[...] = d_all[:, at(c, CHUNK)].T

        def body(n):
            tpart[:, at(n, TILE)] = jnp.dot(dts[...], ph[:, at(n, TILE)], preferred_element_type=f32)
            cs[c, :, at(n, TILE)] = tpart[other, at(n, TILE)].astype(bf16)

        loop(F // TILE, body)
        core_copy(c).start()
        core_copy(c).wait_recv()

        def add(n):
            value = tpart[mine, at(n, CHUNK)] + cr[c, :, at(n, CHUNK)].astype(f32)
            ys[c, :, at(n, CHUNK)] = value.astype(bf16)

        loop(F // CHUNK, add)
        y_copy(c).start()
        scale = tsc[token_rows(c), :]
        acc = jnp.zeros((HC, LANE), f32)
        for k in range(F // LANE):
            lanes = slice(k * LANE, (k + 1) * LANE)
            acc = acc + ts[token_rows(c), lanes].astype(f32) * scale * ys[c, :, lanes].astype(f32)
        als[c] = jnp.broadcast_to(to_row(acc), als.shape[1:])
        for i in range(3):
            along_copy(c, i).start()

    def arrive(c):
        x2_copy(c).wait_recv()
        settle(m2, xr2, c, r2, nr)

    def both(c):
        arrive(c)
        token_product(c)

    x0_copy.wait_recv()
    settle(m1, xr1, 0, r1, rp)
    both(0)
    x1_copy.wait_recv()
    loop(C - 1, lambda i: settle(m1, xr1, i + 1, r1, rp))
    panel_product(r1, rp)

    @pl.when(col == 0)
    def _():
        forward(N - 1, right, None)

    @pl.when(col == N - 1)
    def _():
        forward(0, left, None)

    loop(C - 2, lambda i: both(i + 1))
    arrive(C - 1)
    panel_product(r2, nr)

    @pl.when(col == 0)
    def _():
        for d in range(N - 2, 0, -1):
            forward(d, right, None)

    @pl.when(col == N - 1)
    def _():
        for d in range(1, N - 1):
            forward(d, left, None)

    @pl.when((col > 0) & (col < N // 2))
    def _():
        forward(N - 1, right, zr)

    @pl.when((col < N - 1) & (col >= N // 2))
    def _():
        forward(0, left, zl)

    token_product(C - 1)

    def loss_copy(d, src):
        return remote(lsend.at[d], lrecv.at[src], los.at[d], lor.at[src], {"col": d})

    def loss_rows(d):
        rows = block(d)
        scale = psc[rows, :]
        acc = jnp.zeros((rp, LANE), f32)
        for k in range(F // LANE):
            lanes = slice(k * LANE, (k + 1) * LANE)
            acc = acc + ps[rows, lanes].astype(f32) * scale * part[rows, lanes]
        loss_row = to_row(loss_acc[rows, :])
        along_row = to_row(acc)
        lsend[d, 0:4, :] = jnp.broadcast_to(loss_row, (4, loss_row.shape[1]))
        lsend[d, 4:8, :] = jnp.broadcast_to(along_row, (4, along_row.shape[1]))

    loop(N, loss_rows)
    for k in range(1, N):
        d = (col + k) % N
        loss_copy(d, col).start()

    def token_term(c, lanes):
        return ys[c, :, lanes].astype(f32) + yr[c, :, lanes].astype(f32)

    def gather_copy(c):
        return remote(cr.at[c], gt_o.at[token_rows(c), :], ags.at[c], agr.at[c], cdev)

    def own_copy(c):
        return pltpu.make_async_copy(cr.at[c], gt_o.at[token_rows(c), :], outs.at[c])

    def token_finish(c):
        y_copy(c).wait_recv()
        for i in range(3):
            along_copy(c, i).wait_recv()
        here = als[c, 0:1, :] + alr[c, 1, 0:1, :]
        there = alr[c, 0, 0:1, :] + alr[c, 2, 0:1, :]
        along = to_column(here + there)
        scale = tsc[token_rows(c), :]
        for k in range(F // LANE):
            lanes = slice(k * LANE, (k + 1) * LANE)
            unit = ts[token_rows(c), lanes].astype(f32) * scale
            cr[c, :, lanes] = ((token_term(c, lanes) - unit * along) * scale).astype(bf16)
        gather_copy(c).start()
        own_copy(c).start()

    def chain(k):
        d = N - 1 - k
        go = (col < d) & (col > 0)
        if k == 0:
            go = go & (col >= N // 2)

        @pl.when(go)
        def _():
            forward(d, right, zr)

        e = k
        go = (col > e) & (col < N - 1)
        if k == 0:
            go = go & (col < N // 2)

        @pl.when(go)
        def _():
            forward(e, left, zl)

    for i in range(max(C, N - 1)):
        if i < N - 1:
            chain(i)
        if i == 0:
            total = lsend[col]
            for k in range(1, N):
                src = (col + N - k) % N
                loss_copy(col, src).wait_recv()
                total = total + lrecv[src]
            loss_o[...] = total
            als[C] = total
            along_copy(C, 0).start()
        if i < C:
            token_finish(i)

    own = block(col)

    def absorb(arrived):
        def body(n):
            part[own, at(n, CHUNK)] += arrived[own, at(n, CHUNK)].astype(f32)

        loop(F // CHUNK, body)

    @pl.when(col > 0)
    def _():
        right(col).wait_recv()
        absorb(zr)

    @pl.when(col < N - 1)
    def _():
        left(col).wait_recv()
        absorb(zl)

    scale = psc[own, :]
    along_copy(C, 0).wait_recv()
    along = to_column(als[C, 4:5, :] + alr[C, 0, 4:5, :])[:rp]
    for k in range(F // LANE):
        lanes = slice(k * LANE, (k + 1) * LANE)
        unit = ps[own, lanes].astype(f32) * scale
        gp_o[:, lanes] = ((part[own, lanes] - unit * along) * scale).astype(bf16)

    sq_copy.wait_send()
    x1_copy.wait_send()
    x0_copy.wait_send()

    def ends(c):
        x2_copy(c).wait_send()
        core_copy(c).wait_send()
        y_copy(c).wait_send()
        for i in range(3):
            along_copy(c, i).wait_send()
        gather_copy(c).wait_send()
        gather_copy(c).wait_recv()
        own_copy(c).wait()

    loop(C, ends)
    along_copy(C, 0).wait_send()

    for k in range(1, N):
        d = (col + k) % N
        loss_copy(d, col).wait_send()
        right(d).wait_send()


def hand_over(loss, panel, tokens, loss_o, panel_o, tokens_o, panel_v, tokens_v, sem_in, sem_out):
    loss_o[...] = loss[0, :loss_o.shape[0]]
    moves = [(panel, panel_v, panel_o)]
    for t in range(0, tokens.shape[0], CHUNK):
        rows = pl.ds(t, CHUNK)
        moves.append((tokens.at[rows, :], tokens_v.at[rows, :], tokens_o.at[rows, :]))
    ins = [pltpu.make_async_copy(a, b, sem_in.at[i]) for i, (a, b, _) in enumerate(moves)]
    outs = [pltpu.make_async_copy(b, c, sem_out.at[i]) for i, (_, b, c) in enumerate(moves)]
    for copy in ins:
        copy.start()
    for copy, out in zip(ins, outs):
        copy.wait()
        out.start()
    for out in outs:
        out.wait()


def local(rows_n, cols_n, panel_student, panel_teacher, tokens_student, tokens_teacher):
    Pn, F = panel_student.shape
    T = tokens_student.shape[0]
    N, C = cols_n, T // CHUNK
    rp = Pn // N
    nr, HC, W = Pn - rp, CHUNK // 2, max(Pn, T)
    lp = max(rp, LANE)
    V, S = pltpu.VMEM, pltpu.SemaphoreType.DMA
    scratch = [
        V((Pn, F), bf16), V((Pn, F), bf16), V((T, F), bf16), V((T, F), bf16), V((Pn, F), bf16), V((T, F), bf16),
        V((8, W), f32), V((8, W), f32), V((8, W), f32), V((Pn, LANE), f32), V((Pn, LANE), f32), V((T, LANE), f32),
        V((C, rp, CHUNK), f32), V((rp, CHUNK), f32), V((nr, CHUNK), f32), V((C, nr, CHUNK), f32),
        V((C, rp, CHUNK), bf16), V((C, rp, CHUNK), bf16), V((C, nr, CHUNK), bf16), V((C, nr, CHUNK), bf16),
        V((Pn, T), bf16), V((CHUNK, Pn), bf16),
        V((Pn, LANE), f32), V((N, 8, lp), f32), V((N, 8, lp), f32),
        V((Pn, F), f32), V((Pn, F), bf16), V((Pn, F), bf16), V((Pn, F), bf16),
        V((CHUNK, F), f32), V((C, HC, F), bf16), V((C, HC, F), bf16), V((C, HC, F), bf16), V((C, HC, F), bf16),
        V((C + 1, 8, lp), f32), V((C + 1, 3, 8, lp), f32),
        S((4,)), S((2,)), S((4,)), S((C,)), S((C,)), S((C,)), S((C,)), S((C,)), S((C,)),
        S((N,)), S((N,)), S((N,)), S((N,)), S((N,)), S((C + 1, 3)), S((C + 1, 3)), S((C,)), S((C,)), S((C,)),
    ]
    anywhere, vmem = pl.BlockSpec(memory_space=pl.ANY), pl.BlockSpec(memory_space=pltpu.VMEM)
    loss, grad_panel, grad_tokens = pl.pallas_call(
        functools.partial(kernel, rows_n, cols_n),
        out_shape=(
            jax.ShapeDtypeStruct((8, lp), f32),
            jax.ShapeDtypeStruct((rp, F), bf16),
            jax.ShapeDtypeStruct((T, F), bf16),
        ),
        in_specs=[anywhere] * 4,
        out_specs=(vmem, vmem, anywhere),
        scratch_shapes=scratch,
        compiler_params=pltpu.CompilerParams(
            collective_id=0, has_side_effects=True, vmem_limit_bytes=62 * 1024 * 1024
        ),
    )(panel_student, panel_teacher, tokens_student, tokens_teacher)
    pieces = T // CHUNK + 1
    return pl.pallas_call(
        hand_over,
        out_shape=(
            jax.ShapeDtypeStruct((rp,), f32),
            jax.ShapeDtypeStruct((rp, F), bf16),
            jax.ShapeDtypeStruct((T, F), bf16),
        ),
        in_specs=[vmem, anywhere, anywhere],
        out_specs=(vmem, anywhere, anywhere),
        scratch_shapes=[V((rp, F), bf16), V((T, F), bf16), S((pieces,)), S((pieces,))],
    )(loss, grad_panel, grad_tokens)


def solution(mesh):
    placed = (P("row", "feat"), P("row", "feat"), P("col", "feat"), P("col", "feat"))
    return jax.shard_map(
        functools.partial(local, mesh.shape["row"], mesh.shape["col"]),
        mesh=mesh,
        in_specs=placed,
        out_specs=(P(("row", "col")), P(("row", "col"), "feat"), P("col", "feat")),
        check_vma=False,
    )
```

```python
import functools

import jax
import jax.numpy as jnp
from jax import lax
from jax.experimental import pallas as pl
from jax.experimental.pallas import tpu as pltpu
from jax.sharding import PartitionSpec as P

epsilon = 1e-06
MESH = pl.DeviceIdType.MESH
f32, bf16 = jnp.float32, jnp.bfloat16
LANE = 128
CHUNK = 256
TILE = 1024


def nt(a, b):
    return lax.dot_general(a, b, (((1,), (1,)), ((), ())), preferred_element_type=f32)


def loop(count, body):
    def step(i, carry):
        body(i)
        return carry

    lax.fori_loop(0, count, step, 0)


def at(i, size):
    return pl.ds(pl.multiple_of(i * size, size), size)


def to_row(acc):
    rows = acc.shape[0]
    if rows < LANE:
        acc = jnp.concatenate([acc, jnp.zeros((LANE - rows, LANE), f32)], axis=0)
    return jnp.sum(acc.T, axis=0, keepdims=True)


def to_column(row):
    return jnp.broadcast_to(row, (LANE, row.shape[1])).T


def kernel(
    rows_n, cols_n,
    ps_h, pt_h, ts_h, tt_h,
    loss_o, gp_o, gt_o,
    ps, pt, ts, tt, ph, th,
    sq, sqr, inv, psc, ptc, tsc,
    m1, g1t, m2, xs1, xr1, xs2, xr2, d_all, dts,
    loss_acc, lsend, lrecv,
    part, zs, zr, zl,
    tpart, cs, cr, ys, yr,
    als, alr,
    lsem, sqsem, x1sem, x2s, x2r, cos, cor, yos, yor, zss, zrr, zlr, los, lor, als_s, alr_s, ags, agr, outs,
):
    N = cols_n
    Pn, F = ps.shape
    T = ts.shape[0]
    C = T // CHUNK
    rp = Pn // N
    nr = Pn - rp
    row, col, feat = lax.axis_index("row"), lax.axis_index("col"), lax.axis_index("feat")
    xdev = {"feat": 1 - feat}
    low = row % 2
    cdev = {"row": row + 1 - 2 * low}
    ydev = {"row": row + 2 - 4 * ((row // 2) % 2)}
    first_half = col < N // 2
    r1 = pl.multiple_of(jnp.where(first_half, N - 1, 0) * rp, rp)
    r2 = pl.multiple_of(jnp.where(first_half, 0, 1) * rp, rp)
    HC = CHUNK // 2

    loads = [
        pltpu.make_async_copy(h, v, lsem.at[i])
        for i, (h, v) in enumerate(((ps_h, ps), (ts_h, ts), (pt_h, pt), (tt_h, tt)))
    ]
    for load in loads:
        load.start()

    barrier = pltpu.get_barrier_semaphore()
    for dev in (xdev, cdev, ydev):
        pl.semaphore_signal(barrier, inc=1, device_id=dev, device_id_type=MESH)
    for k in range(1, N):
        pl.semaphore_signal(barrier, inc=1, device_id={"col": (col + k) % N}, device_id_type=MESH)
    pl.semaphore_wait(barrier, 3 + N - 1)

    def remote(src, dst, s, r, dev):
        return pltpu.make_async_remote_copy(
            src_ref=src, dst_ref=dst, send_sem=s, recv_sem=r, device_id=dev, device_id_type=MESH
        )

    sq[...] = jnp.zeros_like(sq)

    def squares(ref, i, count):
        def body(t):
            acc = jnp.zeros((LANE, LANE), f32)
            for k in range(F // LANE):
                v = ref[at(t, LANE), k * LANE:(k + 1) * LANE].astype(f32)
                acc = acc + v * v
            sq[i:i + 1, at(t, LANE)] = to_row(acc)

        loop(count // LANE, body)

    for load, (ref, i, count) in zip(loads, ((ps, 0, Pn), (ts, 2, T), (pt, 1, Pn), (tt, 3, T))):
        load.wait()
        squares(ref, i, count)
    sq_copy = remote(sq, sqr, sqsem.at[0], sqsem.at[1], xdev)
    sq_copy.start()

    def raw(c):
        m1[c] = nt(ps[pl.ds(r1, rp), :], ts[at(c, CHUNK), :])
        g1t[c] = nt(pt[pl.ds(r1, rp), :], tt[at(c, CHUNK), :])

    loop(C, raw)
    sq_copy.wait_recv()
    inv[...] = 1.0 / jnp.sqrt(sq[...] + sqr[...] + epsilon)
    for i, ref in ((0, psc), (1, ptc), (2, tsc)):
        for t in range(ref.shape[0] // LANE):
            ref[t * LANE:(t + 1) * LANE, :] = to_column(inv[i:i + 1, t * LANE:(t + 1) * LANE])

    def scaled(gs, gt, c, r0, count, m_ref, s_ref):
        for j in range(CHUNK // LANE):
            lanes = slice(j * LANE, (j + 1) * LANE)
            where = pl.ds(pl.multiple_of(c * CHUNK + j * LANE, LANE), LANE)
            m = gs[:, lanes] * psc[pl.ds(r0, count), :] * inv[2:3, where]
            m = m - gt[:, lanes] * ptc[pl.ds(r0, count), :] * inv[3:4, where]
            m_ref[c, :, lanes] = m
            s_ref[c, :, lanes] = m.astype(bf16)

    loop(C, lambda c: scaled(m1[c], g1t[c], c, r1, rp, m1, xs1))
    x1_copy = remote(xs1, xr1, x1sem.at[0], x1sem.at[1], xdev)
    x1_copy.start()

    def x2_copy(c):
        return remote(xs2.at[c], xr2.at[c], x2s.at[c], x2r.at[c], xdev)

    def rest(c):
        gs = nt(ps[pl.ds(r2, nr), :], ts[at(c, CHUNK), :])
        gt = nt(pt[pl.ds(r2, nr), :], tt[at(c, CHUNK), :])
        scaled(gs, gt, c, r2, nr, m2, xs2)
        x2_copy(c).start()

    loop(C, rest)

    def halves(src, column, dst):
        def body(t):
            scale = column[at(t, LANE), :]
            for k in range(F // LANE):
                lanes = slice(k * LANE, (k + 1) * LANE)
                dst[at(t, LANE), lanes] = (src[at(t, LANE), lanes].astype(f32) * scale).astype(bf16)

        loop(src.shape[0] // LANE, body)

    halves(ts, tsc, th)
    halves(ps, psc, ph)

    loss_acc[...] = jnp.zeros_like(loss_acc)

    def settle(m_ref, x_ref, c, r0, count):
        for j in range(CHUNK // LANE):
            lanes = slice(j * LANE, (j + 1) * LANE)
            m = m_ref[c, :, lanes] + x_ref[c, :, lanes].astype(f32)
            where = pl.ds(pl.multiple_of(c * CHUNK + j * LANE, LANE), LANE)
            d_all[pl.ds(r0, count), where] = (2.0 * m).astype(bf16)
            loss_acc[pl.ds(r0, count), :] += m * m

    def panel_product(r0, count):
        def body(n):
            part[pl.ds(r0, count), at(n, TILE)] = jnp.dot(
                d_all[pl.ds(r0, count), :], th[:, at(n, TILE)], preferred_element_type=f32
            )

        loop(F // TILE, body)

    def block(d):
        return pl.ds(pl.multiple_of(d * rp, rp), rp)

    def right(d):
        return remote(zs.at[block(d), :], zr.at[block(d), :], zss.at[d], zrr.at[d], {"col": (col + 1) % N})

    def left(d):
        return remote(zs.at[block(d), :], zl.at[block(d), :], zss.at[d], zlr.at[d], {"col": (col + N - 1) % N})

    def forward(d, copy, arrived):
        def body(n):
            value = part[block(d), at(n, CHUNK)]
            if arrived is not None:
                value = value + arrived[block(d), at(n, CHUNK)].astype(f32)
            zs[block(d), at(n, CHUNK)] = value.astype(bf16)

        if arrived is not None:
            copy(d).wait_recv()
        loop(F // CHUNK, body)
        copy(d).start()

    x1_copy.wait_recv()
    loop(C, lambda c: settle(m1, xr1, c, r1, rp))
    panel_product(r1, rp)

    @pl.when(col == 0)
    def _():
        forward(N - 1, right, None)

    @pl.when(col == N - 1)
    def _():
        forward(0, left, None)

    def core_copy(c):
        return remote(cs.at[c], cr.at[c], cos.at[c], cor.at[c], cdev)

    def y_copy(c):
        return remote(ys.at[c], yr.at[c], yos.at[c], yor.at[c], ydev)

    mine = pl.ds(pl.multiple_of(low * HC, HC), HC)
    other = pl.ds(pl.multiple_of((1 - low) * HC, HC), HC)

    def token_product(c):
        dts[...] = d_all[:, at(c, CHUNK)].T

        def body(n):
            tpart[:, at(n, TILE)] = jnp.dot(dts[...], ph[:, at(n, TILE)], preferred_element_type=f32)
            cs[c, :, at(n, TILE)] = tpart[other, at(n, TILE)].astype(bf16)

        loop(F // TILE, body)
        core_copy(c).start()
        core_copy(c).wait_recv()

        def add(n):
            value = tpart[mine, at(n, CHUNK)] + cr[c, :, at(n, CHUNK)].astype(f32)
            ys[c, :, at(n, CHUNK)] = value.astype(bf16)

        loop(F // CHUNK, add)
        y_copy(c).start()

    def arrive(c):
        x2_copy(c).wait_recv()
        settle(m2, xr2, c, r2, nr)

    def both(c):
        arrive(c)
        token_product(c)

    loop(C - 1, both)
    arrive(C - 1)
    panel_product(r2, nr)

    @pl.when(col == 0)
    def _():
        for d in range(N - 2, 0, -1):
            forward(d, right, None)

    @pl.when(col == N - 1)
    def _():
        for d in range(1, N - 1):
            forward(d, left, None)

    @pl.when((col > 0) & (col < N // 2))
    def _():
        forward(N - 1, right, zr)

    @pl.when((col < N - 1) & (col >= N // 2))
    def _():
        forward(0, left, zl)

    token_product(C - 1)

    def loss_copy(d, src):
        return remote(lsend.at[d], lrecv.at[src], los.at[d], lor.at[src], {"col": d})

    def loss_rows(d):
        lsend[d] = jnp.broadcast_to(to_row(loss_acc[block(d), :]), lsend.shape[1:])

    loop(N, loss_rows)
    for k in range(1, N):
        d = (col + k) % N
        loss_copy(d, col).start()

    def along_copy(i):
        return remote(als.at[i], alr.at[i], als_s.at[i], alr_s.at[i], xdev)

    def token_rows(c):
        return pl.ds(pl.multiple_of(c * CHUNK + low * HC, HC), HC)

    def token_term(c, lanes):
        return ys[c, :, lanes].astype(f32) + yr[c, :, lanes].astype(f32)

    def token_along(c):
        y_copy(c).wait_recv()
        scale = tsc[token_rows(c), :]
        acc = jnp.zeros((HC, LANE), f32)
        for k in range(F // LANE):
            lanes = slice(k * LANE, (k + 1) * LANE)
            acc = acc + ts[token_rows(c), lanes].astype(f32) * scale * token_term(c, lanes)
        als[c] = jnp.broadcast_to(to_row(acc), als.shape[1:])
        along_copy(c).start()

    def gather_copy(c):
        return remote(cr.at[c], gt_o.at[token_rows(c), :], ags.at[c], agr.at[c], cdev)

    def own_copy(c):
        return pltpu.make_async_copy(cr.at[c], gt_o.at[token_rows(c), :], outs.at[c])

    def token_finish(c):
        along_copy(c).wait_recv()
        along = to_column(als[c, 0:1, :] + alr[c, 0:1, :])
        scale = tsc[token_rows(c), :]
        for k in range(F // LANE):
            lanes = slice(k * LANE, (k + 1) * LANE)
            unit = ts[token_rows(c), lanes].astype(f32) * scale
            cr[c, :, lanes] = ((token_term(c, lanes) - unit * along) * scale).astype(bf16)
        gather_copy(c).start()
        own_copy(c).start()

    def chain(k):
        d = N - 1 - k
        go = (col < d) & (col > 0)
        if k == 0:
            go = go & (col >= N // 2)

        @pl.when(go)
        def _():
            forward(d, right, zr)

        e = k
        go = (col > e) & (col < N - 1)
        if k == 0:
            go = go & (col < N // 2)

        @pl.when(go)
        def _():
            forward(e, left, zl)

    for i in range(max(C, N - 1)):
        if i < N - 1:
            chain(i)
        if i < C:
            token_along(i)
        if 0 < i < C:
            token_finish(i - 1)

    own = block(col)

    def absorb(arrived):
        def body(n):
            part[own, at(n, CHUNK)] += arrived[own, at(n, CHUNK)].astype(f32)

        loop(F // CHUNK, body)

    @pl.when(col > 0)
    def _():
        right(col).wait_recv()
        absorb(zr)

    @pl.when(col < N - 1)
    def _():
        left(col).wait_recv()
        absorb(zl)

    scale = psc[own, :]
    acc = jnp.zeros((rp, LANE), f32)
    for k in range(F // LANE):
        lanes = slice(k * LANE, (k + 1) * LANE)
        acc = acc + ps[own, lanes].astype(f32) * scale * part[own, lanes]
    als[C] = jnp.broadcast_to(to_row(acc), als.shape[1:])
    along_copy(C).start()
    token_finish(C - 1)
    total = lsend[col]
    for k in range(1, N):
        src = (col + N - k) % N
        loss_copy(col, src).wait_recv()
        total = total + lrecv[src]
    loss_o[...] = total
    along_copy(C).wait_recv()
    along = to_column(als[C, 0:1, :] + alr[C, 0:1, :])[:rp]
    for k in range(F // LANE):
        lanes = slice(k * LANE, (k + 1) * LANE)
        unit = ps[own, lanes].astype(f32) * scale
        gp_o[:, lanes] = ((part[own, lanes] - unit * along) * scale).astype(bf16)

    sq_copy.wait_send()
    x1_copy.wait_send()

    def ends(c):
        x2_copy(c).wait_send()
        core_copy(c).wait_send()
        y_copy(c).wait_send()
        along_copy(c).wait_send()
        gather_copy(c).wait_send()
        gather_copy(c).wait_recv()
        own_copy(c).wait()

    loop(C, ends)
    along_copy(C).wait_send()

    for k in range(1, N):
        d = (col + k) % N
        loss_copy(d, col).wait_send()
        right(d).wait_send()


def hand_over(loss, panel, tokens, loss_o, panel_o, tokens_o, panel_v, tokens_v, sem_in, sem_out):
    loss_o[...] = loss[0, :loss_o.shape[0]]
    moves = [(panel, panel_v, panel_o)]
    for t in range(0, tokens.shape[0], CHUNK):
        rows = pl.ds(t, CHUNK)
        moves.append((tokens.at[rows, :], tokens_v.at[rows, :], tokens_o.at[rows, :]))
    ins = [pltpu.make_async_copy(a, b, sem_in.at[i]) for i, (a, b, _) in enumerate(moves)]
    outs = [pltpu.make_async_copy(b, c, sem_out.at[i]) for i, (_, b, c) in enumerate(moves)]
    for copy in ins:
        copy.start()
    for copy, out in zip(ins, outs):
        copy.wait()
        out.start()
    for out in outs:
        out.wait()


def local(rows_n, cols_n, panel_student, panel_teacher, tokens_student, tokens_teacher):
    Pn, F = panel_student.shape
    T = tokens_student.shape[0]
    N, C = cols_n, T // CHUNK
    rp = Pn // N
    nr, HC, W = Pn - rp, CHUNK // 2, max(Pn, T)
    lp = max(rp, LANE)
    V, S = pltpu.VMEM, pltpu.SemaphoreType.DMA
    scratch = [
        V((Pn, F), bf16), V((Pn, F), bf16), V((T, F), bf16), V((T, F), bf16), V((Pn, F), bf16), V((T, F), bf16),
        V((8, W), f32), V((8, W), f32), V((8, W), f32), V((Pn, LANE), f32), V((Pn, LANE), f32), V((T, LANE), f32),
        V((C, rp, CHUNK), f32), V((C, rp, CHUNK), f32), V((C, nr, CHUNK), f32),
        V((C, rp, CHUNK), bf16), V((C, rp, CHUNK), bf16), V((C, nr, CHUNK), bf16), V((C, nr, CHUNK), bf16),
        V((Pn, T), bf16), V((CHUNK, Pn), bf16),
        V((Pn, LANE), f32), V((N, 8, lp), f32), V((N, 8, lp), f32),
        V((Pn, F), f32), V((Pn, F), bf16), V((Pn, F), bf16), V((Pn, F), bf16),
        V((CHUNK, F), f32), V((C, HC, F), bf16), V((C, HC, F), bf16), V((C, HC, F), bf16), V((C, HC, F), bf16),
        V((C + 1, 8, lp), f32), V((C + 1, 8, lp), f32),
        S((4,)), S((2,)), S((2,)), S((C,)), S((C,)), S((C,)), S((C,)), S((C,)), S((C,)),
        S((N,)), S((N,)), S((N,)), S((N,)), S((N,)), S((C + 1,)), S((C + 1,)), S((C,)), S((C,)), S((C,)),
    ]
    anywhere, vmem = pl.BlockSpec(memory_space=pl.ANY), pl.BlockSpec(memory_space=pltpu.VMEM)
    loss, grad_panel, grad_tokens = pl.pallas_call(
        functools.partial(kernel, rows_n, cols_n),
        out_shape=(
            jax.ShapeDtypeStruct((8, lp), f32),
            jax.ShapeDtypeStruct((rp, F), bf16),
            jax.ShapeDtypeStruct((T, F), bf16),
        ),
        in_specs=[anywhere] * 4,
        out_specs=(vmem, vmem, anywhere),
        scratch_shapes=scratch,
        compiler_params=pltpu.CompilerParams(
            collective_id=0, has_side_effects=True, vmem_limit_bytes=62 * 1024 * 1024
        ),
    )(panel_student, panel_teacher, tokens_student, tokens_teacher)
    pieces = T // CHUNK + 1
    return pl.pallas_call(
        hand_over,
        out_shape=(
            jax.ShapeDtypeStruct((rp,), f32),
            jax.ShapeDtypeStruct((rp, F), bf16),
            jax.ShapeDtypeStruct((T, F), bf16),
        ),
        in_specs=[vmem, anywhere, anywhere],
        out_specs=(vmem, anywhere, anywhere),
        scratch_shapes=[V((rp, F), bf16), V((T, F), bf16), S((pieces,)), S((pieces,))],
    )(loss, grad_panel, grad_tokens)


def solution(mesh):
    placed = (P("row", "feat"), P("row", "feat"), P("col", "feat"), P("col", "feat"))
    return jax.shard_map(
        functools.partial(local, mesh.shape["row"], mesh.shape["col"]),
        mesh=mesh,
        in_specs=placed,
        out_specs=(P(("row", "col")), P(("row", "col"), "feat"), P("col", "feat")),
        check_vma=False,
    )
```
